32 devices in a mesh: groups: 2 (over x), item: 8 (over z, y), user: 2 (over core).
Axes of the slice: x: 2, y: 2, z: 4, core: 2. Of those that a mesh axis runs over, the one named last changes fastest.
Arguments:
- interactions: bfloat16 [4096, 8192], P(('groups', 'user'), 'item'), parts along dimension 0, may hold values from 0 to 2, as said below
- counts: int32 [16384], P('groups'), parts along dimension 0, may hold values from 512 to 2048
Outputs:
- similarity: float32 [16384, 8192], P(('groups', 'item', 'user')), parts along dimension 0
The draws below stay inside these ranges and needn't reach their ends.
There are 2 independent parts, one for each index of `groups`. The reference program is written for one: setup_inputs(seed, part) draws one part's arguments, and reference() takes and returns one part's arrays. A program takes and returns all parts, laid end to end along the dimension named above; each array names one. Nothing has to cross between parts.
Inputs may be any that keep to these rules, and one draw needn't show every extreme that they name: `interactions`: about half of the entries are zero; the others lie between 0.25 and 2.
All inputs are finite; a program needn't handle non-finite values.
Results may differ from the reference program's by a relative error of at most 0.0003.
Values may be sent and summed in bfloat16 or wider, within the bound.
A program may use at most 128 MiB of HBM per device.

```python
import jax
import jax.numpy as jnp
from jax import lax

ITEMS = 8192
USERS = 2048


def draw_interactions(key, part):
    key = jax.random.fold_in(key, 11)
    live_key, value_key = jax.random.split(key)
    live = jax.random.bernoulli(live_key, 0.5, (USERS, ITEMS))
    spread = jax.random.uniform(value_key, (USERS, ITEMS), jnp.float32)
    values = 0.25 + 1.75 * spread
    return jnp.where(live, values, 0.0).astype(jnp.bfloat16)


def place_ends(entries, stream_key, least, largest):
    shape = entries.shape
    spot = [jax.random.randint(jax.random.fold_in(stream_key, axis), (), 0, shape[axis]) for axis in range(len(shape))]
    entries = entries.at[tuple(spot)].set(least)
    longest = shape.index(max(shape))
    spot[longest] = (spot[longest] + 1) % shape[longest]
    return entries.at[tuple(spot)].set(largest)


def setup_inputs(seed: int = 0, part: int = 0) -> dict:
    arg_keys = jax.random.split(jax.random.key(seed), 3)
    part_keys = jax.random.split(jax.random.fold_in(arg_keys[2], part), 3)
    return {
        "interactions": draw_interactions(jax.random.fold_in(jax.random.fold_in(arg_keys[2], part), 71), part),
        "counts": place_ends(jax.random.randint(part_keys[1], (ITEMS,), USERS // 4, USERS + 1), jax.random.fold_in(part_keys[1], 1), USERS // 4, USERS).astype(jnp.int32),
    }


def reference(interactions, counts):
    co_counts = lax.dot_general(interactions, interactions, (((0,), (0,)), ((), ())), preferred_element_type=jnp.float32)
    count_float = counts.astype(jnp.float32)
    return co_counts * (count_float ** -0.4)[:, None] * (count_float ** -0.6)[None, :]
```

```python
import functools

import jax
import jax.numpy as jnp
from jax import lax
from jax.experimental import pallas as pl
from jax.experimental.pallas import tpu as pltpu
from jax.sharding import PartitionSpec as P

MESH = pl.DeviceIdType.MESH
PIECES = 4


def kernel(nz, ny, x_ref, row_ref, col_ref, out_ref, panel, left, made,
           got, got_core, sent_down, sent_up, sent_side, sent_core, placed, loaded):
    users, block = x_ref.shape
    half = out_ref.shape[0]
    rows = users // PIECES
    split = PIECES // 2
    group = lax.axis_index("groups")
    me = lax.axis_index("item")
    core = lax.axis_index("user")
    z, y = me // ny, me % ny
    base = core * users

    def at(zz, yy):
        return (group, zz * ny + yy, core)

    down, up, side = at(z - 1, y), at(z + 1, y), at(z, ny - 1 - y)
    other = (group, me, 1 - core)
    not_first, not_last = z > 0, z < nz - 1

    barrier = pltpu.get_barrier_semaphore()
    pl.semaphore_signal(barrier, inc=1, device_id=other, device_id_type=MESH)
    if ny > 1:
        pl.semaphore_signal(barrier, inc=1, device_id=side, device_id_type=MESH)

    @pl.when(not_first)
    def _():
        pl.semaphore_signal(barrier, inc=1, device_id=down, device_id_type=MESH)

    @pl.when(not_last)
    def _():
        pl.semaphore_signal(barrier, inc=1, device_id=up, device_id_type=MESH)

    load = pltpu.make_async_copy(x_ref, panel.at[me, pl.ds(base, users)], loaded)
    load.start()
    wanted = ny + jnp.where(not_first, 1, 0) + jnp.where(not_last, 1, 0)
    pl.semaphore_wait(barrier, wanted)

    def place(b, p):
        return panel.at[b, pl.ds(pl.multiple_of(base + p * rows, rows), rows)]

    def send(b, p, sems, recv, device, source=None):
        pltpu.make_async_remote_copy(
            src_ref=place(b, p) if source is None else source,
            dst_ref=place(b, p),
            send_sem=sems.at[b],
            recv_sem=recv,
            device_id=device,
            device_id_type=MESH,
        ).start()

    def take(b, p):
        pltpu.make_async_copy(place(b, p), place(b, p), got.at[b, p]).wait()

    def to_down(b, p, source=None):
        @pl.when(not_first)
        def _():
            send(b, p, sent_down, got.at[b, p], down, source)

    def to_up(b, p, source=None):
        @pl.when(not_last)
        def _():
            send(b, p, sent_up, got.at[b, p], up, source)

    def to_side(b, p, source=None):
        send(b, p, sent_side, got.at[b, p], side, source)

    def to_core(b, p, source=None):
        send(b, p, sent_core, got_core.at[b], other, source)

    for p in range(PIECES):
        mine = x_ref.at[pl.ds(p * rows, rows)]
        to_down(me, p, mine)
        to_up(me, p, mine)
        if ny > 1:
            to_side(me, p, mine)
        to_core(me, p, mine)

    def whole(b, sem, start, count):
        piece = panel.at[b, pl.ds(start, count)]
        pltpu.make_async_copy(piece, piece, sem).wait()

    def take_core(b):
        whole(b, got_core.at[b], (1 - core) * users, users)

    tile = min(256, block)

    def product(b):
        def columns(c, _):
            cols = pl.ds(pl.multiple_of(c * tile, tile), tile)
            co = jnp.dot(left[...], panel[b, :, cols], preferred_element_type=jnp.float32)
            made[b, :, cols] = co * row_ref[...] * col_ref[b, :, cols]
            return 0

        lax.fori_loop(0, block // tile, columns, 0)
        result(b).start()

    def result(b):
        return pltpu.make_async_copy(
            made.at[b], out_ref.at[:, pl.ds(pl.multiple_of(b * block, block), block)], placed.at[b])

    load.wait()
    take_core(me)
    quarter = min(256, users)

    def turn(c, _):
        part = pl.ds(pl.multiple_of(c * quarter, quarter), quarter)
        own = panel[me, part, pl.ds(pl.multiple_of(core * half, half), half)]
        left[:, part] = own.astype(jnp.float32).T.astype(left.dtype)
        return 0

    lax.fori_loop(0, 2 * users // quarter, turn, 0)
    product(me)

    def step(s, _):
        t, p = s // PIECES, s % PIECES

        def along(zb, onward):
            b = zb * ny + y

            @pl.when(jnp.logical_and(zb >= 0, zb < nz))
            def _():
                take(b, p)
                onward(b, p)
                if ny > 1:
                    @pl.when(jnp.logical_or(t > 0, p >= split))
                    def _():
                        to_side(b, p)
                to_core(b, p)

        along(z + 1 + t, to_down)
        along(z - 1 - t, to_up)
        if ny > 1:
            b0 = z * ny + (ny - 1 - y)

            @pl.when(t == 0)
            def _():
                take(b0, p)

                @pl.when(p < split)
                def _():
                    to_down(b0, p)
                    to_up(b0, p)

                to_core(b0, p)

            def crossed(zb):
                @pl.when(jnp.logical_and(t > 0, jnp.logical_and(zb >= 0, zb < nz)))
                def _():
                    b = zb * ny + (ny - 1 - y)
                    take(b, p)
                    to_core(b, p)

            crossed(z + t)
            crossed(z - t)

        kinds = 4 if ny > 1 else 2
        tt = t - 1
        back, crossing = p % 2, p // 2
        zb = z + (1 - 2 * back) * (tt + 1 - crossing)
        yb = y + crossing * (ny - 1 - 2 * y)
        fits = jnp.logical_and(zb >= 0, zb < nz)
        first = jnp.logical_and(p < kinds, jnp.logical_or(tt > 0, jnp.logical_and(tt == 0, p < 3)))

        @pl.when(jnp.logical_and(fits, first))
        def _():
            b = zb * ny + yb
            take_core(b)
            product(b)

        return 0

    lax.fori_loop(0, (nz + 1) * PIECES, step, 0)

    def drain(b, _):
        zb, yb = b // ny, b % ny
        result(b).wait()
        whole(b, sent_core.at[b], base, users)
        straight = yb == y

        @pl.when(jnp.logical_and(straight, jnp.logical_and(zb >= z, not_first)))
        def _():
            whole(b, sent_down.at[b], base, users)

        @pl.when(jnp.logical_and(straight, jnp.logical_and(zb <= z, not_last)))
        def _():
            whole(b, sent_up.at[b], base, users)

        if ny > 1:
            layer = jnp.logical_and(jnp.logical_not(straight), zb == z)
            near = jnp.logical_or(zb == z + 1, zb == z - 1)

            @pl.when(jnp.logical_and(layer, not_first))
            def _():
                whole(b, sent_down.at[b], base, split * rows)

            @pl.when(jnp.logical_and(layer, not_last))
            def _():
                whole(b, sent_up.at[b], base, split * rows)

            @pl.when(jnp.logical_and(straight, near))
            def _():
                whole(b, sent_side.at[b], base, (PIECES - split) * rows)

            @pl.when(jnp.logical_and(straight, jnp.logical_not(near)))
            def _():
                whole(b, sent_side.at[b], base, users)

        return 0

    lax.fori_loop(0, nz * ny, drain, 0)


def shards(nz, ny, interactions, counts):
    users, block = interactions.shape
    n = nz * ny
    half = block // lax.axis_size("user")
    count_float = counts.astype(jnp.float32)
    start = lax.axis_index("item") * block + lax.axis_index("user") * half
    row_damp = (lax.dynamic_slice_in_dim(count_float, start, half) ** (-0.4))[:, None]
    col_damp = (count_float ** (-0.6)).reshape(n, 1, block)
    dma = pltpu.SemaphoreType.DMA
    return pl.pallas_call(
        functools.partial(kernel, nz, ny),
        out_shape=jax.ShapeDtypeStruct((half, n * block), jnp.float32),
        in_specs=[
            pl.BlockSpec(memory_space=pl.ANY),
            pl.BlockSpec(memory_space=pltpu.VMEM),
            pl.BlockSpec(memory_space=pltpu.VMEM),
        ],
        out_specs=pl.BlockSpec(memory_space=pl.ANY),
        scratch_shapes=[
            pltpu.VMEM((n, 2 * users, block), interactions.dtype),
            pltpu.VMEM((half, 2 * users), interactions.dtype),
            pltpu.VMEM((n, half, block), jnp.float32),
            dma((n, PIECES)),
            dma((n,)),
            dma((n,)),
            dma((n,)),
            dma((n,)),
            dma((n,)),
            dma((n,)),
            dma,
        ],
        compiler_params=pltpu.CompilerParams(
            collective_id=0, has_side_effects=True, vmem_limit_bytes=60 * 1024 * 1024
        ),
        cost_estimate=pl.CostEstimate(
            flops=4 * half * users * n * block, bytes_accessed=4 * half * n * block, transcendentals=0
        ),
    )(interactions, row_damp, col_damp)


def columns_of(mesh):
    n = mesh.shape["item"]
    spots = [getattr(d, "coords", None) for d in mesh.devices[0, :, 0]]
    if any(spot is None for spot in spots):
        return 1
    ny = len({spot[1] for spot in spots})
    return ny if ny == 2 and n % 2 == 0 else 1


def solution(mesh):
    ny = columns_of(mesh)
    placed = (P(("groups", "user"), "item"), P("groups"))
    return jax.shard_map(
        functools.partial(shards, mesh.shape["item"] // ny, ny),
        mesh=mesh,
        in_specs=placed,
        out_specs=P(("groups", "item", "user"), None),
        check_vma=False,
    )
```

```python
import functools

import jax
import jax.numpy as jnp
from jax import lax
from jax.experimental import pallas as pl
from jax.experimental.pallas import tpu as pltpu
from jax.sharding import PartitionSpec as P

MESH = pl.DeviceIdType.MESH
PIECES = 8


def kernel(nz, ny, x_ref, counts_ref, out_ref, panel, left, row_damp, col_damp,
           got, got_core, sent_down, sent_up, sent_side, sent_core, loaded):
    users, block = x_ref.shape
    half = out_ref.shape[0]
    rows = users // PIECES
    split = PIECES // 2
    group = lax.axis_index("groups")
    me = lax.axis_index("item")
    core = lax.axis_index("user")
    z, y = me // ny, me % ny
    base = core * users

    def at(zz, yy):
        return (group, zz * ny + yy, core)

    down, up, side = at(z - 1, y), at(z + 1, y), at(z, ny - 1 - y)
    other = (group, me, 1 - core)
    not_first, not_last = z > 0, z < nz - 1

    barrier = pltpu.get_barrier_semaphore()
    pl.semaphore_signal(barrier, inc=1, device_id=other, device_id_type=MESH)
    if ny > 1:
        pl.semaphore_signal(barrier, inc=1, device_id=side, device_id_type=MESH)

    @pl.when(not_first)
    def _():
        pl.semaphore_signal(barrier, inc=1, device_id=down, device_id_type=MESH)

    @pl.when(not_last)
    def _():
        pl.semaphore_signal(barrier, inc=1, device_id=up, device_id_type=MESH)

    load = pltpu.make_async_copy(x_ref, panel.at[me, pl.ds(base, users)], loaded)
    load.start()
    wanted = ny + jnp.where(not_first, 1, 0) + jnp.where(not_last, 1, 0)
    pl.semaphore_wait(barrier, wanted)

    def place(b, p):
        return panel.at[b, pl.ds(pl.multiple_of(base + p * rows, rows), rows)]

    def send(b, p, sems, recv, device, source=None):
        pltpu.make_async_remote_copy(
            src_ref=place(b, p) if source is None else source,
            dst_ref=place(b, p),
            send_sem=sems.at[b],
            recv_sem=recv,
            device_id=device,
            device_id_type=MESH,
        ).start()

    def take(b, p):
        pltpu.make_async_copy(place(b, p), place(b, p), got.at[b, p]).wait()

    def to_down(b, p, source=None):
        @pl.when(not_first)
        def _():
            send(b, p, sent_down, got.at[b, p], down, source)

    def to_up(b, p, source=None):
        @pl.when(not_last)
        def _():
            send(b, p, sent_up, got.at[b, p], up, source)

    def to_side(b, p, source=None):
        send(b, p, sent_side, got.at[b, p], side, source)

    def to_core(b, p, source=None):
        send(b, p, sent_core, got_core.at[b], other, source)

    for p in range(PIECES):
        mine = x_ref.at[pl.ds(p * rows, rows)]
        to_down(me, p, mine)
        to_up(me, p, mine)
        if ny > 1:
            to_side(me, p, mine)
        to_core(me, p, mine)

    def whole(b, sem, start, count):
        piece = panel.at[b, pl.ds(start, count)]
        pltpu.make_async_copy(piece, piece, sem).wait()

    def take_core(b):
        whole(b, got_core.at[b], (1 - core) * users, users)

    tile = min(256, block)

    def product(b):
        def columns(c, _):
            cols = pl.ds(pl.multiple_of(c * tile, tile), tile)
            co = jnp.dot(left[...], panel[b, :, cols], preferred_element_type=jnp.float32)
            spot = pl.ds(pl.multiple_of(b * block + c * tile, tile), tile)
            out_ref[:, spot] = co * row_damp[:, :1] * col_damp[b, :, cols]
            return 0

        lax.fori_loop(0, block // tile, columns, 0)

    logs = jnp.log(counts_ref[...].astype(jnp.float32))
    col_damp[...] = jnp.exp(-0.6 * logs)
    mine = counts_ref[me, :, pl.ds(pl.multiple_of(core * half, half), half)].astype(jnp.float32)
    row_damp[...] = jnp.broadcast_to(jnp.exp(-0.4 * jnp.log(mine)), (128, half)).T
    load.wait()
    take_core(me)
    quarter = min(256, users)

    def turn(c, _):
        part = pl.ds(pl.multiple_of(c * quarter, quarter), quarter)
        own = panel[me, part, pl.ds(pl.multiple_of(core * half, half), half)]
        left[:, part] = own.astype(jnp.float32).T.astype(left.dtype)
        return 0

    lax.fori_loop(0, 2 * users // quarter, turn, 0)
    product(me)

    def step(s, _):
        t, p = s // PIECES, s % PIECES

        def along(zb, onward):
            b = zb * ny + y

            @pl.when(jnp.logical_and(zb >= 0, zb < nz))
            def _():
                take(b, p)
                onward(b, p)
                if ny > 1:
                    @pl.when(jnp.logical_or(t > 0, p >= split))
                    def _():
                        to_side(b, p)
                to_core(b, p)

        along(z + 1 + t, to_down)
        along(z - 1 - t, to_up)
        if ny > 1:
            b0 = z * ny + (ny - 1 - y)

            @pl.when(t == 0)
            def _():
                take(b0, p)

                @pl.when(p < split)
                def _():
                    to_down(b0, p)
                    to_up(b0, p)

                to_core(b0, p)

            def crossed(zb):
                @pl.when(jnp.logical_and(t > 0, jnp.logical_and(zb >= 0, zb < nz)))
                def _():
                    b = zb * ny + (ny - 1 - y)
                    take(b, p)
                    to_core(b, p)

            crossed(z + t)
            crossed(z - t)

        kinds = 4 if ny > 1 else 2
        tt = t - 1
        kind = p // (PIECES // 4)
        back, crossing = kind % 2, kind // 2
        zb = z + (1 - 2 * back) * (tt + 1 - crossing)
        yb = y + crossing * (ny - 1 - 2 * y)
        fits = jnp.logical_and(zb >= 0, zb < nz)
        turn_now = jnp.logical_and(p % (PIECES // 4) == 0, kind < kinds)
        first = jnp.logical_and(turn_now, jnp.logical_or(tt > 0, jnp.logical_and(tt == 0, kind < 3)))

        @pl.when(jnp.logical_and(fits, first))
        def _():
            b = zb * ny + yb
            take_core(b)
            product(b)

        return 0

    lax.fori_loop(0, (nz + 1) * PIECES, step, 0)

    def drain(b, _):
        zb, yb = b // ny, b % ny
        whole(b, sent_core.at[b], base, users)
        straight = yb == y

        @pl.when(jnp.logical_and(straight, jnp.logical_and(zb >= z, not_first)))
        def _():
            whole(b, sent_down.at[b], base, users)

        @pl.when(jnp.logical_and(straight, jnp.logical_and(zb <= z, not_last)))
        def _():
            whole(b, sent_up.at[b], base, users)

        if ny > 1:
            layer = jnp.logical_and(jnp.logical_not(straight), zb == z)
            near = jnp.logical_or(zb == z + 1, zb == z - 1)

            @pl.when(jnp.logical_and(layer, not_first))
            def _():
                whole(b, sent_down.at[b], base, split * rows)

            @pl.when(jnp.logical_and(layer, not_last))
            def _():
                whole(b, sent_up.at[b], base, split * rows)

            @pl.when(jnp.logical_and(straight, near))
            def _():
                whole(b, sent_side.at[b], base, (PIECES - split) * rows)

            @pl.when(jnp.logical_and(straight, jnp.logical_not(near)))
            def _():
                whole(b, sent_side.at[b], base, users)

        return 0

    lax.fori_loop(0, nz * ny, drain, 0)


def shards(nz, ny, interactions, counts):
    users, block = interactions.shape
    n = nz * ny
    half = block // lax.axis_size("user")
    dma = pltpu.SemaphoreType.DMA
    return pl.pallas_call(
        functools.partial(kernel, nz, ny),
        out_shape=pltpu.VMEM((half, n * block), jnp.float32),
        in_specs=[
            pl.BlockSpec(memory_space=pl.ANY),
            pl.BlockSpec(memory_space=pltpu.VMEM),
        ],
        out_specs=pl.BlockSpec(memory_space=pltpu.VMEM),
        scratch_shapes=[
            pltpu.VMEM((n, 2 * users, block), interactions.dtype),
            pltpu.VMEM((half, 2 * users), interactions.dtype),
            pltpu.VMEM((half, 128), jnp.float32),
            pltpu.VMEM((n, 1, block), jnp.float32),
            dma((n, PIECES)),
            dma((n,)),
            dma((n,)),
            dma((n,)),
            dma((n,)),
            dma((n,)),
            dma,
        ],
        compiler_params=pltpu.CompilerParams(
            collective_id=0, has_side_effects=True, vmem_limit_bytes=40 * 1024 * 1024
        ),
        cost_estimate=pl.CostEstimate(
            flops=4 * half * users * n * block, bytes_accessed=4 * half * n * block, transcendentals=0
        ),
    )(interactions, counts.reshape(n, 1, block))


def columns_of(mesh):
    n = mesh.shape["item"]
    spots = [getattr(d, "coords", None) for d in mesh.devices[0, :, 0]]
    if any(spot is None for spot in spots):
        return 1
    ny = len({spot[1] for spot in spots})
    return ny if ny == 2 and n % 2 == 0 else 1


def solution(mesh):
    ny = columns_of(mesh)
    placed = (P(("groups", "user"), "item"), P("groups"))
    return jax.shard_map(
        functools.partial(shards, mesh.shape["item"] // ny, ny),
        mesh=mesh,
        in_specs=placed,
        out_specs=P(("groups", "item", "user"), None),
        check_vma=False,
    )
```

```python
import functools

import jax
import jax.numpy as jnp
from jax import lax
from jax.experimental import pallas as pl
from jax.experimental.pallas import tpu as pltpu
from jax.sharding import PartitionSpec as P

MESH = pl.DeviceIdType.MESH
PIECES = 8
LEVELS = 32767


def has_far(nz, ny):
    return nz == 4 and ny == 2


def kernel(nz, ny, x_ref, counts_ref, out_ref, panel, left, row_damp, col_damp,
           got, got_core, sent_down, sent_up, sent_side, sent_core, loaded, *remote):
    users, block = x_ref.shape
    half = out_ref.shape[0]
    rows = users // PIECES
    split = PIECES // 2
    group = lax.axis_index("groups")
    me = lax.axis_index("item")
    core = lax.axis_index("user")
    z, y = me // ny, me % ny
    base = core * users

    def at(zz, yy):
        return (group, zz * ny + yy, core)

    down, up, side = at(z - 1, y), at(z + 1, y), at(z, ny - 1 - y)
    other = (group, me, 1 - core)
    not_first, not_last = z > 0, z < nz - 1
    far = has_far(nz, ny)
    reach = nz - 2 if far else nz - 1
    is_end = jnp.logical_or(z == 0, z == nz - 1)
    is_middle = jnp.logical_not(is_end)
    near_end = jnp.where(z < 2, 0, nz - 1)
    far_end = nz - 1 - near_end
    if far:
        left_far, sums, scales, sent_sums, got_sums, sent_scales, got_scales = remote

    barrier = pltpu.get_barrier_semaphore()
    pl.semaphore_signal(barrier, inc=1, device_id=other, device_id_type=MESH)
    if ny > 1:
        pl.semaphore_signal(barrier, inc=1, device_id=side, device_id_type=MESH)

    @pl.when(not_first)
    def _():
        pl.semaphore_signal(barrier, inc=1, device_id=down, device_id_type=MESH)

    @pl.when(not_last)
    def _():
        pl.semaphore_signal(barrier, inc=1, device_id=up, device_id_type=MESH)

    load = pltpu.make_async_copy(x_ref, panel.at[me, pl.ds(base, users)], loaded)
    load.start()
    wanted = ny + jnp.where(not_first, 1, 0) + jnp.where(not_last, 1, 0)
    pl.semaphore_wait(barrier, wanted)

    def place(b, p):
        return panel.at[b, pl.ds(pl.multiple_of(base + p * rows, rows), rows)]

    def send(b, p, sems, recv, device, source=None):
        pltpu.make_async_remote_copy(
            src_ref=place(b, p) if source is None else source,
            dst_ref=place(b, p),
            send_sem=sems.at[b],
            recv_sem=recv,
            device_id=device,
            device_id_type=MESH,
        ).start()

    def take(b, p):
        pltpu.make_async_copy(place(b, p), place(b, p), got.at[b, p]).wait()

    def to_down(b, p, source=None):
        @pl.when(not_first)
        def _():
            send(b, p, sent_down, got.at[b, p], down, source)

    def to_up(b, p, source=None):
        @pl.when(not_last)
        def _():
            send(b, p, sent_up, got.at[b, p], up, source)

    def to_side(b, p, source=None):
        send(b, p, sent_side, got.at[b, p], side, source)

    def to_core(b, p, source=None):
        send(b, p, sent_core, got_core.at[b], other, source)

    for p in range(PIECES):
        mine = x_ref.at[pl.ds(p * rows, rows)]
        to_down(me, p, mine)
        to_up(me, p, mine)
        if ny > 1:
            to_side(me, p, mine)
        to_core(me, p, mine)

    def whole(b, sem, start, count):
        piece = panel.at[b, pl.ds(start, count)]
        pltpu.make_async_copy(piece, piece, sem).wait()

    def take_core(b):
        whole(b, got_core.at[b], (1 - core) * users, users)

    tile = min(256, block)

    def product(b):
        def columns(c, _):
            cols = pl.ds(pl.multiple_of(c * tile, tile), tile)
            co = jnp.dot(left[...], panel[b, :, cols], preferred_element_type=jnp.float32)
            spot = pl.ds(pl.multiple_of(b * block + c * tile, tile), tile)
            out_ref[:, spot] = co * row_damp[:, :1] * col_damp[b, :, cols]
            return 0

        lax.fori_loop(0, block // tile, columns, 0)

    logs = jnp.log(counts_ref[...].astype(jnp.float32))
    col_damp[...] = jnp.exp(-0.6 * logs)
    mine = counts_ref[me, :, pl.ds(pl.multiple_of(core * half, half), half)].astype(jnp.float32)
    row_damp[...] = jnp.broadcast_to(jnp.exp(-0.4 * jnp.log(mine)), (128, half)).T
    load.wait()
    take_core(me)
    quarter = min(256, users)

    def turned(b, target):
        def turn(c, _):
            part = pl.ds(pl.multiple_of(c * quarter, quarter), quarter)
            own = panel[b, part, pl.ds(pl.multiple_of(core * half, half), half)]
            target[:, part] = own.astype(jnp.float32).T.astype(target.dtype)
            return 0

        lax.fori_loop(0, 2 * users // quarter, turn, 0)

    turned(me, left)
    product(me)
    tiles = block // tile

    def far_block(k):
        return far_end * ny + y + k * (ny - 1 - 2 * y)

    def sums_copy(k, c):
        return pltpu.make_async_remote_copy(
            src_ref=sums.at[k, c], dst_ref=sums.at[k, c], send_sem=sent_sums.at[k], recv_sem=got_sums.at[k],
            device_id=at(near_end, y), device_id_type=MESH)

    def scales_copy(k):
        return pltpu.make_async_remote_copy(
            src_ref=scales.at[k], dst_ref=scales.at[k], send_sem=sent_scales.at[k], recv_sem=got_scales.at[k],
            device_id=at(near_end, y), device_id_type=MESH)

    def send_sums(k, _):
        b = far_block(k)
        take_core(b)
        scales[k] = jnp.zeros((8, half), jnp.float32)

        def columns(c, _):
            cols = pl.ds(pl.multiple_of(c * tile, tile), tile)
            co = jnp.dot(left_far[...], panel[b, :, cols], preferred_element_type=jnp.float32)
            most = jnp.maximum(jnp.max(co, axis=1, keepdims=True), 1e-30)
            level = (co * (2 * LEVELS / most) + 0.5).astype(jnp.int32) - LEVELS
            sums[k, c] = level.astype(jnp.int16)
            unit = jnp.broadcast_to(most * (0.5 / LEVELS), (half, 128)).T
            scales[k, pl.ds(c, 1), :] = unit[0:1]
            sums_copy(k, c).start()
            return 0

        lax.fori_loop(0, tiles, columns, 0)
        scales_copy(k).start()
        return 0

    def take_sums(k, _):
        b = far_end_of_end() * ny + y + k * (ny - 1 - 2 * y)
        pltpu.make_async_copy(sums.at[k], sums.at[k], got_sums.at[k]).wait()
        pltpu.make_async_copy(scales.at[k], scales.at[k], got_scales.at[k]).wait()

        def columns(c, _):
            cols = pl.ds(pl.multiple_of(c * tile, tile), tile)
            unit = jnp.broadcast_to(scales[k, pl.ds(c, 1), :], (128, half)).T
            level = sums[k, c].astype(jnp.int32) + LEVELS
            co = level.astype(jnp.float32) * unit[:, :1]
            spot = pl.ds(pl.multiple_of(b * block + c * tile, tile), tile)
            out_ref[:, spot] = co * row_damp[:, :1] * col_damp[b, :, cols]
            return 0

        lax.fori_loop(0, tiles, columns, 0)
        return 0

    def far_end_of_end():
        return nz - 1 - z

    def distance(t):
        return jnp.where(is_middle, 3 - t, t) if far else t

    def reached(t):
        return jnp.logical_and(t >= 1, t <= reach)

    def step(s, _):
        t, p = s // PIECES, s % PIECES

        def along(zb, onward):
            b = zb * ny + y

            @pl.when(jnp.logical_and(t < reach, jnp.logical_and(zb >= 0, zb < nz)))
            def _():
                take(b, p)

                @pl.when(t + 2 <= reach)
                def _():
                    onward(b, p)

                if ny > 1:
                    across = jnp.logical_or(t > 0, is_end if far else p >= split)

                    @pl.when(across)
                    def _():
                        to_side(b, p)
                to_core(b, p)

        along(z + 1 + t, to_down)
        along(z - 1 - t, to_up)
        if ny > 1:
            b0 = z * ny + (ny - 1 - y)

            @pl.when(t == 0)
            def _():
                take(b0, p)

                if not far:
                    @pl.when(p < split)
                    def _():
                        to_down(b0, p)
                        to_up(b0, p)

                to_core(b0, p)

            if far:
                @pl.when(jnp.logical_and(s == PIECES, is_middle))
                def _():
                    def inward(q, _):
                        @pl.when(z == 1)
                        def _():
                            to_up(b0, q)

                        @pl.when(z == 2)
                        def _():
                            to_down(b0, q)

                        return 0

                    lax.fori_loop(0, PIECES, inward, 0)

                @pl.when(jnp.logical_and(s == 2 * PIECES - 1, is_middle))
                def _():
                    def late(q, _):
                        to_side(near_end * ny + y, q)
                        return 0

                    lax.fori_loop(0, PIECES, late, 0)

            lag = 1 if far else 0
            tc, pc = (s + PIECES - lag) // PIECES - 1, (s + PIECES - lag) % PIECES

            def crossed(zb):
                @pl.when(jnp.logical_and(reached(tc), jnp.logical_and(zb >= 0, zb < nz)))
                def _():
                    b = zb * ny + (ny - 1 - y)
                    take(b, pc)
                    to_core(b, pc)

            crossed(z + distance(tc))
            crossed(z - distance(tc))

        if far:
            @pl.when(jnp.logical_and(s == 2 * PIECES - 2, is_middle))
            def _():
                turned(near_end * ny + y, left_far)

            @pl.when(jnp.logical_and(s == 2 * PIECES, is_middle))
            def _():
                lax.fori_loop(0, 2, send_sums, 0)

        kinds = 4 if ny > 1 else 2
        tt = t - 1
        kind = p // (PIECES // 4)
        back, crossing = kind % 2, kind // 2
        gap = jnp.where(crossing == 1, jnp.where(tt == 0, 0, distance(tt)), tt + 1)
        zb = z + (1 - 2 * back) * gap
        yb = y + crossing * (ny - 1 - 2 * y)
        fits = jnp.logical_and(jnp.logical_and(zb >= 0, zb < nz), jnp.logical_and(gap <= reach, tt <= reach))
        turn_now = jnp.logical_and(p % (PIECES // 4) == 0, kind < kinds)
        first = jnp.logical_and(turn_now, jnp.logical_or(tt > 0, jnp.logical_and(tt == 0, kind < 3)))

        @pl.when(jnp.logical_and(fits, first))
        def _():
            b = zb * ny + yb
            if far:
                @pl.when(jnp.logical_or(is_end, tt != 1))
                def _():
                    take_core(b)
            else:
                take_core(b)
            product(b)

        return 0

    lax.fori_loop(0, (reach + 2) * PIECES, step, 0)
    if far:
        @pl.when(is_end)
        def _():
            lax.fori_loop(0, 2, take_sums, 0)

        @pl.when(is_middle)
        def _():
            for k in range(2):
                pltpu.make_async_copy(sums.at[k], sums.at[k], sent_sums.at[k]).wait()
                pltpu.make_async_copy(scales.at[k], scales.at[k], sent_scales.at[k]).wait()

    def drain(b, _):
        zb, yb = b // ny, b % ny
        straight = yb == y
        here = jnp.logical_and(zb - z <= reach, z - zb <= reach)

        @pl.when(here)
        def _():
            whole(b, sent_core.at[b], base, users)

        falls = jnp.logical_and(zb >= z, zb - z + 1 <= reach)
        rises = jnp.logical_and(zb <= z, z - zb + 1 <= reach)

        @pl.when(jnp.logical_and(straight, jnp.logical_and(falls, not_first)))
        def _():
            whole(b, sent_down.at[b], base, users)

        @pl.when(jnp.logical_and(straight, jnp.logical_and(rises, not_last)))
        def _():
            whole(b, sent_up.at[b], base, users)

        if far:
            layer = jnp.logical_and(jnp.logical_not(straight), zb == z)

            @pl.when(jnp.logical_and(layer, z == 2))
            def _():
                whole(b, sent_down.at[b], base, users)

            @pl.when(jnp.logical_and(layer, z == 1))
            def _():
                whole(b, sent_up.at[b], base, users)

            inner = jnp.logical_and(is_middle, zb == nz - 1 - z)

            @pl.when(jnp.logical_and(jnp.logical_and(straight, here), jnp.logical_not(inner)))
            def _():
                whole(b, sent_side.at[b], base, users)

        elif ny > 1:
            layer = jnp.logical_and(jnp.logical_not(straight), zb == z)
            near = jnp.logical_or(zb == z + 1, zb == z - 1)

            @pl.when(jnp.logical_and(layer, not_first))
            def _():
                whole(b, sent_down.at[b], base, split * rows)

            @pl.when(jnp.logical_and(layer, not_last))
            def _():
                whole(b, sent_up.at[b], base, split * rows)

            @pl.when(jnp.logical_and(straight, near))
            def _():
                whole(b, sent_side.at[b], base, (PIECES - split) * rows)

            @pl.when(jnp.logical_and(straight, jnp.logical_not(near)))
            def _():
                whole(b, sent_side.at[b], base, users)

        return 0

    lax.fori_loop(0, nz * ny, drain, 0)


def shards(nz, ny, interactions, counts):
    users, block = interactions.shape
    n = nz * ny
    half = block // lax.axis_size("user")
    dma = pltpu.SemaphoreType.DMA
    tile = min(256, block)
    remote = [
        pltpu.VMEM((half, 2 * users), interactions.dtype),
        pltpu.VMEM((2, block // tile, half, tile), jnp.int16),
        pltpu.VMEM((2, 8, half), jnp.float32),
        dma((2,)),
        dma((2,)),
        dma((2,)),
        dma((2,)),
    ] if has_far(n // ny, ny) else []
    return pl.pallas_call(
        functools.partial(kernel, nz, ny),
        out_shape=pltpu.VMEM((half, n * block), jnp.float32),
        in_specs=[
            pl.BlockSpec(memory_space=pl.ANY),
            pl.BlockSpec(memory_space=pltpu.VMEM),
        ],
        out_specs=pl.BlockSpec(memory_space=pltpu.VMEM),
        scratch_shapes=[
            pltpu.VMEM((n, 2 * users, block), interactions.dtype),
            pltpu.VMEM((half, 2 * users), interactions.dtype),
            pltpu.VMEM((half, 128), jnp.float32),
            pltpu.VMEM((n, 1, block), jnp.float32),
            dma((n, PIECES)),
            dma((n,)),
            dma((n,)),
            dma((n,)),
            dma((n,)),
            dma((n,)),
            dma,
            *remote,
        ],
        compiler_params=pltpu.CompilerParams(
            collective_id=0, has_side_effects=True, vmem_limit_bytes=(44 if remote else 40) * 1024 * 1024
        ),
        cost_estimate=pl.CostEstimate(
            flops=4 * half * users * n * block, bytes_accessed=4 * half * n * block, transcendentals=0
        ),
    )(interactions, counts.reshape(n, 1, block))


def columns_of(mesh):
    n = mesh.shape["item"]
    spots = [getattr(d, "coords", None) for d in mesh.devices[0, :, 0]]
    if any(spot is None for spot in spots):
        return 1
    ny = len({spot[1] for spot in spots})
    return ny if ny == 2 and n % 2 == 0 else 1


def solution(mesh):
    ny = columns_of(mesh)
    placed = (P(("groups", "user"), "item"), P("groups"))
    return jax.shard_map(
        functools.partial(shards, mesh.shape["item"] // ny, ny),
        mesh=mesh,
        in_specs=placed,
        out_specs=P(("groups", "item", "user"), None),
        check_vma=False,
    )
```

```python
import functools

import jax
import jax.numpy as jnp
from jax import lax
from jax.experimental import pallas as pl
from jax.experimental.pallas import tpu as pltpu
from jax.sharding import PartitionSpec as P

MESH = pl.DeviceIdType.MESH
PIECES = 8
LEVELS = 32767


def has_far(nz, ny):
    return nz == 4 and ny == 2


def kernel(nz, ny, x_ref, counts_ref, out_ref, panel, left, row_damp, col_damp,
           got, got_core, sent_down, sent_up, sent_side, sent_core, loaded, *remote):
    users, block = x_ref.shape
    half = out_ref.shape[0]
    rows = users // PIECES
    split = PIECES // 2
    group = lax.axis_index("groups")
    me = lax.axis_index("item")
    core = lax.axis_index("user")
    z, y = me // ny, me % ny
    base = core * users

    def at(zz, yy):
        return (group, zz * ny + yy, core)

    down, up, side = at(z - 1, y), at(z + 1, y), at(z, ny - 1 - y)
    other = (group, me, 1 - core)
    not_first, not_last = z > 0, z < nz - 1
    far = has_far(nz, ny)
    reach = nz - 2 if far else nz - 1
    is_end = jnp.logical_or(z == 0, z == nz - 1)
    is_middle = jnp.logical_not(is_end)
    near_end = jnp.where(z < 2, 0, nz - 1)
    far_end = nz - 1 - near_end
    if far:
        left_far, sums, scales, sent_sums, got_sums, sent_scales, got_scales = remote

    barrier = pltpu.get_barrier_semaphore()
    pl.semaphore_signal(barrier, inc=1, device_id=other, device_id_type=MESH)
    if ny > 1:
        pl.semaphore_signal(barrier, inc=1, device_id=side, device_id_type=MESH)

    @pl.when(not_first)
    def _():
        pl.semaphore_signal(barrier, inc=1, device_id=down, device_id_type=MESH)

    @pl.when(not_last)
    def _():
        pl.semaphore_signal(barrier, inc=1, device_id=up, device_id_type=MESH)

    load = pltpu.make_async_copy(x_ref, panel.at[me, pl.ds(base, users)], loaded)
    load.start()
    wanted = ny + jnp.where(not_first, 1, 0) + jnp.where(not_last, 1, 0)
    pl.semaphore_wait(barrier, wanted)

    def place(b, p):
        return panel.at[b, pl.ds(pl.multiple_of(base + p * rows, rows), rows)]

    def send(b, p, sems, recv, device, source=None):
        pltpu.make_async_remote_copy(
            src_ref=place(b, p) if source is None else source,
            dst_ref=place(b, p),
            send_sem=sems.at[b],
            recv_sem=recv,
            device_id=device,
            device_id_type=MESH,
        ).start()

    def take(b, p):
        pltpu.make_async_copy(place(b, p), place(b, p), got.at[b, p]).wait()

    def to_down(b, p, source=None):
        @pl.when(not_first)
        def _():
            send(b, p, sent_down, got.at[b, p], down, source)

    def to_up(b, p, source=None):
        @pl.when(not_last)
        def _():
            send(b, p, sent_up, got.at[b, p], up, source)

    def to_side(b, p, source=None):
        send(b, p, sent_side, got.at[b, p], side, source)

    def to_core(b, p, source=None):
        send(b, p, sent_core, got_core.at[b], other, source)

    for p in range(PIECES):
        mine = x_ref.at[pl.ds(p * rows, rows)]
        to_down(me, p, mine)
        to_up(me, p, mine)
        if ny > 1:
            to_side(me, p, mine)
        to_core(me, p, mine)

    def whole(b, sem, start, count):
        piece = panel.at[b, pl.ds(start, count)]
        pltpu.make_async_copy(piece, piece, sem).wait()

    def take_core(b):
        whole(b, got_core.at[b], (1 - core) * users, users)

    tile = min(256, block)

    def product(b):
        def columns(c, _):
            cols = pl.ds(pl.multiple_of(c * tile, tile), tile)
            co = jnp.dot(left[...], panel[b, :, cols], preferred_element_type=jnp.float32)
            spot = pl.ds(pl.multiple_of(b * block + c * tile, tile), tile)
            out_ref[:, spot] = co * row_damp[:, :1] * col_damp[b, :, cols]
            return 0

        lax.fori_loop(0, block // tile, columns, 0)

    logs = jnp.log(counts_ref[...].astype(jnp.float32))
    col_damp[...] = jnp.exp(-0.6 * logs)
    mine = counts_ref[me, :, pl.ds(pl.multiple_of(core * half, half), half)].astype(jnp.float32)
    row_damp[...] = jnp.broadcast_to(jnp.exp(-0.4 * jnp.log(mine)), (128, half)).T
    load.wait()
    take_core(me)
    quarter = min(256, users)

    def turned(b, target):
        def turn(c, _):
            part = pl.ds(pl.multiple_of(c * quarter, quarter), quarter)
            own = panel[b, part, pl.ds(pl.multiple_of(core * half, half), half)]
            target[:, part] = own.astype(jnp.float32).T.astype(target.dtype)
            return 0

        lax.fori_loop(0, 2 * users // quarter, turn, 0)

    turned(me, left)
    product(me)
    tiles = block // tile

    def far_block(k):
        return far_end * ny + y + k * (ny - 1 - 2 * y)

    def sums_copy(k, c):
        return pltpu.make_async_remote_copy(
            src_ref=sums.at[k, c], dst_ref=sums.at[k, c], send_sem=sent_sums.at[k], recv_sem=got_sums.at[k],
            device_id=at(near_end, y), device_id_type=MESH)

    def scales_copy(k):
        return pltpu.make_async_remote_copy(
            src_ref=scales.at[k], dst_ref=scales.at[k], send_sem=sent_scales.at[k], recv_sem=got_scales.at[k],
            device_id=at(near_end, y), device_id_type=MESH)

    def send_sums(k, _):
        b = far_block(k)
        take_core(b)
        scales[k] = jnp.zeros((8, half), jnp.float32)

        def columns(c, _):
            cols = pl.ds(pl.multiple_of(c * tile, tile), tile)
            co = jnp.dot(left_far[...], panel[b, :, cols], preferred_element_type=jnp.float32)
            most = jnp.maximum(jnp.max(co, axis=1, keepdims=True), 1e-30)
            level = (co * (2 * LEVELS / most) + 0.5).astype(jnp.int32) - LEVELS
            sums[k, c] = level.astype(jnp.int16)
            unit = jnp.broadcast_to(most * (0.5 / LEVELS), (half, 128)).T
            scales[k, pl.ds(c, 1), :] = unit[0:1]
            sums_copy(k, c).start()
            return 0

        lax.fori_loop(0, tiles, columns, 0)
        scales_copy(k).start()
        return 0

    def take_sums(k, _):
        b = far_end_of_end() * ny + y + k * (ny - 1 - 2 * y)
        pltpu.make_async_copy(sums.at[k], sums.at[k], got_sums.at[k]).wait()
        pltpu.make_async_copy(scales.at[k], scales.at[k], got_scales.at[k]).wait()

        def columns(c, _):
            cols = pl.ds(pl.multiple_of(c * tile, tile), tile)
            unit = jnp.broadcast_to(scales[k, pl.ds(c, 1), :], (128, half)).T
            level = sums[k, c].astype(jnp.int32) + LEVELS
            co = level.astype(jnp.float32) * unit[:, :1]
            spot = pl.ds(pl.multiple_of(b * block + c * tile, tile), tile)
            out_ref[:, spot] = co * row_damp[:, :1] * col_damp[b, :, cols]
            return 0

        lax.fori_loop(0, tiles, columns, 0)
        return 0

    def far_end_of_end():
        return nz - 1 - z

    def distance(t):
        return jnp.where(is_middle, 3 - t, t) if far else t

    def reached(t):
        return jnp.logical_and(t >= 1, t <= reach)

    def step(s, _):
        t, p = s // PIECES, s % PIECES

        def along(zb, onward):
            b = zb * ny + y

            @pl.when(jnp.logical_and(t < reach, jnp.logical_and(zb >= 0, zb < nz)))
            def _():
                take(b, p)

                @pl.when(t + 2 <= reach)
                def _():
                    onward(b, p)

                if ny > 1:
                    across = jnp.logical_or(t > 0, is_end if far else p >= split)

                    @pl.when(across)
                    def _():
                        to_side(b, p)
                to_core(b, p)

        along(z + 1 + t, to_down)
        along(z - 1 - t, to_up)
        if ny > 1:
            b0 = z * ny + (ny - 1 - y)

            @pl.when(t == 0)
            def _():
                take(b0, p)

                if far:
                    @pl.when(z == 0)
                    def _():
                        to_up(b0, p)

                    @pl.when(z == nz - 1)
                    def _():
                        to_down(b0, p)
                else:
                    @pl.when(p < split)
                    def _():
                        to_down(b0, p)
                        to_up(b0, p)

                to_core(b0, p)

            if far:
                @pl.when(jnp.logical_and(s == PIECES, is_middle))
                def _():
                    def inward(q, _):
                        @pl.when(z == 1)
                        def _():
                            to_up(b0, q)

                        @pl.when(z == 2)
                        def _():
                            to_down(b0, q)

                        return 0

                    lax.fori_loop(0, split, inward, 0)

                @pl.when(jnp.logical_and(s == 2 * PIECES - 1, is_middle))
                def _():
                    def late(q, _):
                        to_side((nz - 1 - z) * ny + y, q)
                        return 0

                    lax.fori_loop(split, PIECES, late, 0)

            lag = 1 if far else 0
            tc, pc = (s + PIECES - lag) // PIECES - 1, (s + PIECES - lag) % PIECES

            def crossed(zb):
                @pl.when(jnp.logical_and(reached(tc), jnp.logical_and(zb >= 0, zb < nz)))
                def _():
                    b = zb * ny + (ny - 1 - y)
                    take(b, pc)
                    to_core(b, pc)

            crossed(z + distance(tc))
            crossed(z - distance(tc))

        if far:
            @pl.when(jnp.logical_and(s == 2 * PIECES - 2, is_middle))
            def _():
                turned(near_end * ny + y, left_far)

            @pl.when(jnp.logical_and(jnp.logical_or(s == 2 * PIECES - 1, s == 2 * PIECES), is_middle))
            def _():
                send_sums(s - (2 * PIECES - 1), 0)

        kinds = 4 if ny > 1 else 2
        tt = t - 1
        kind = p // (PIECES // 4)
        back, crossing = kind % 2, kind // 2
        gap = jnp.where(crossing == 1, jnp.where(tt == 0, 0, distance(tt)), tt + 1)
        zb = z + (1 - 2 * back) * gap
        yb = y + crossing * (ny - 1 - 2 * y)
        fits = jnp.logical_and(jnp.logical_and(zb >= 0, zb < nz), jnp.logical_and(gap <= reach, tt <= reach))
        turn_now = jnp.logical_and(p % (PIECES // 4) == 0, kind < kinds)
        first = jnp.logical_and(turn_now, jnp.logical_or(tt > 0, jnp.logical_and(tt == 0, kind < 3)))

        @pl.when(jnp.logical_and(fits, first))
        def _():
            b = zb * ny + yb
            if far:
                @pl.when(jnp.logical_or(is_end, tt != 1))
                def _():
                    take_core(b)
            else:
                take_core(b)
            product(b)

        return 0

    lax.fori_loop(0, (reach + 2) * PIECES, step, 0)
    if far:
        @pl.when(is_end)
        def _():
            lax.fori_loop(0, 2, take_sums, 0)

        @pl.when(is_middle)
        def _():
            for k in range(2):
                pltpu.make_async_copy(sums.at[k], sums.at[k], sent_sums.at[k]).wait()
                pltpu.make_async_copy(scales.at[k], scales.at[k], sent_scales.at[k]).wait()

    def drain(b, _):
        zb, yb = b // ny, b % ny
        straight = yb == y
        here = jnp.logical_and(zb - z <= reach, z - zb <= reach)

        @pl.when(here)
        def _():
            whole(b, sent_core.at[b], base, users)

        falls = jnp.logical_and(zb >= z, zb - z + 1 <= reach)
        rises = jnp.logical_and(zb <= z, z - zb + 1 <= reach)

        @pl.when(jnp.logical_and(straight, jnp.logical_and(falls, not_first)))
        def _():
            whole(b, sent_down.at[b], base, users)

        @pl.when(jnp.logical_and(straight, jnp.logical_and(rises, not_last)))
        def _():
            whole(b, sent_up.at[b], base, users)

        if far:
            layer = jnp.logical_and(jnp.logical_not(straight), zb == z)

            for towards, sems in ((z >= 2, sent_down), (z < 2, sent_up)):

                @pl.when(jnp.logical_and(layer, jnp.logical_and(is_end, towards)))
                def _():
                    whole(b, sems.at[b], base, users)

                @pl.when(jnp.logical_and(layer, jnp.logical_and(is_middle, towards)))
                def _():
                    whole(b, sems.at[b], base, split * rows)

            inner = jnp.logical_and(is_middle, zb == nz - 1 - z)
            outer = jnp.logical_and(is_middle, zb == near_end)
            plain = jnp.logical_not(jnp.logical_or(inner, outer))

            @pl.when(jnp.logical_and(jnp.logical_and(straight, here), plain))
            def _():
                whole(b, sent_side.at[b], base, users)

            @pl.when(jnp.logical_and(straight, inner))
            def _():
                whole(b, sent_side.at[b], base, (PIECES - split) * rows)

        elif ny > 1:
            layer = jnp.logical_and(jnp.logical_not(straight), zb == z)
            near = jnp.logical_or(zb == z + 1, zb == z - 1)

            @pl.when(jnp.logical_and(layer, not_first))
            def _():
                whole(b, sent_down.at[b], base, split * rows)

            @pl.when(jnp.logical_and(layer, not_last))
            def _():
                whole(b, sent_up.at[b], base, split * rows)

            @pl.when(jnp.logical_and(straight, near))
            def _():
                whole(b, sent_side.at[b], base, (PIECES - split) * rows)

            @pl.when(jnp.logical_and(straight, jnp.logical_not(near)))
            def _():
                whole(b, sent_side.at[b], base, users)

        return 0

    lax.fori_loop(0, nz * ny, drain, 0)


def shards(nz, ny, interactions, counts):
    users, block = interactions.shape
    n = nz * ny
    half = block // lax.axis_size("user")
    dma = pltpu.SemaphoreType.DMA
    tile = min(256, block)
    remote = [
        pltpu.VMEM((half, 2 * users), interactions.dtype),
        pltpu.VMEM((2, block // tile, half, tile), jnp.int16),
        pltpu.VMEM((2, 8, half), jnp.float32),
        dma((2,)),
        dma((2,)),
        dma((2,)),
        dma((2,)),
    ] if has_far(n // ny, ny) else []
    return pl.pallas_call(
        functools.partial(kernel, nz, ny),
        out_shape=pltpu.VMEM((half, n * block), jnp.float32),
        in_specs=[
            pl.BlockSpec(memory_space=pl.ANY),
            pl.BlockSpec(memory_space=pltpu.VMEM),
        ],
        out_specs=pl.BlockSpec(memory_space=pltpu.VMEM),
        scratch_shapes=[
            pltpu.VMEM((n, 2 * users, block), interactions.dtype),
            pltpu.VMEM((half, 2 * users), interactions.dtype),
            pltpu.VMEM((half, 128), jnp.float32),
            pltpu.VMEM((n, 1, block), jnp.float32),
            dma((n, PIECES)),
            dma((n,)),
            dma((n,)),
            dma((n,)),
            dma((n,)),
            dma((n,)),
            dma,
            *remote,
        ],
        compiler_params=pltpu.CompilerParams(
            collective_id=0, has_side_effects=True, vmem_limit_bytes=(44 if remote else 40) * 1024 * 1024
        ),
        cost_estimate=pl.CostEstimate(
            flops=4 * half * users * n * block, bytes_accessed=4 * half * n * block, transcendentals=0
        ),
    )(interactions, counts.reshape(n, 1, block))


def columns_of(mesh):
    n = mesh.shape["item"]
    spots = [getattr(d, "coords", None) for d in mesh.devices[0, :, 0]]
    if any(spot is None for spot in spots):
        return 1
    ny = len({spot[1] for spot in spots})
    return ny if ny == 2 and n % 2 == 0 else 1


def solution(mesh):
    ny = columns_of(mesh)
    placed = (P(("groups", "user"), "item"), P("groups"))
    return jax.shard_map(
        functools.partial(shards, mesh.shape["item"] // ny, ny),
        mesh=mesh,
        in_specs=placed,
        out_specs=P(("groups", "item", "user"), None),
        check_vma=False,
    )
```

```python
import functools

import jax
import jax.numpy as jnp
from jax import lax
from jax.experimental import pallas as pl
from jax.experimental.pallas import tpu as pltpu
from jax.sharding import PartitionSpec as P

MESH = pl.DeviceIdType.MESH
PIECES = 4
LEVELS = 32767


def has_far(nz, ny):
    return nz == 4 and ny == 2


def kernel(nz, ny, x_ref, counts_ref, out_ref, panel, left, row_damp, col_damp,
           got, got_core, sent_down, sent_up, sent_side, sent_core, loaded, *remote):
    users, block = x_ref.shape
    half = out_ref.shape[0]
    tile = block // PIECES
    split = PIECES // 2
    group = lax.axis_index("groups")
    me = lax.axis_index("item")
    core = lax.axis_index("user")
    z, y = me // ny, me % ny
    base = core * users

    def at(zz, yy):
        return (group, zz * ny + yy, core)

    down, up, side = at(z - 1, y), at(z + 1, y), at(z, ny - 1 - y)
    other = (group, me, 1 - core)
    not_first, not_last = z > 0, z < nz - 1
    far = has_far(nz, ny)
    reach = nz - 2 if far else nz - 1
    is_end = jnp.logical_or(z == 0, z == nz - 1)
    is_middle = jnp.logical_not(is_end)
    near_end = jnp.where(z < 2, 0, nz - 1)
    far_end = nz - 1 - near_end
    if far:
        left_far, sums, scales, sent_sums, got_sums, sent_scales, got_scales = remote

    barrier = pltpu.get_barrier_semaphore()
    pl.semaphore_signal(barrier, inc=1, device_id=other, device_id_type=MESH)
    if ny > 1:
        pl.semaphore_signal(barrier, inc=1, device_id=side, device_id_type=MESH)

    @pl.when(not_first)
    def _():
        pl.semaphore_signal(barrier, inc=1, device_id=down, device_id_type=MESH)

    @pl.when(not_last)
    def _():
        pl.semaphore_signal(barrier, inc=1, device_id=up, device_id_type=MESH)

    loads = [
        pltpu.make_async_copy(x_ref.at[:, pl.ds(p * tile, tile)], panel.at[me, p, pl.ds(base, users)], loaded.at[p])
        for p in range(PIECES)
    ]
    for load in loads:
        load.start()
    wanted = ny + jnp.where(not_first, 1, 0) + jnp.where(not_last, 1, 0)
    pl.semaphore_wait(barrier, wanted)

    def place(b, p):
        return panel.at[b, p, pl.ds(base, users)]

    def send(b, p, sems, recv, device, source=None):
        pltpu.make_async_remote_copy(
            src_ref=place(b, p) if source is None else source,
            dst_ref=place(b, p),
            send_sem=sems.at[b],
            recv_sem=recv,
            device_id=device,
            device_id_type=MESH,
        ).start()

    def take(b, p):
        pltpu.make_async_copy(place(b, p), place(b, p), got.at[b, p]).wait()

    def to_down(b, p, source=None):
        @pl.when(not_first)
        def _():
            send(b, p, sent_down, got.at[b, p], down, source)

    def to_up(b, p, source=None):
        @pl.when(not_last)
        def _():
            send(b, p, sent_up, got.at[b, p], up, source)

    def to_side(b, p, source=None):
        send(b, p, sent_side, got.at[b, p], side, source)

    def to_core(b, p, source=None):
        send(b, p, sent_core, got_core.at[b, p], other, source)

    for p in range(PIECES):
        mine = x_ref.at[:, pl.ds(p * tile, tile)]
        to_down(me, p, mine)
        to_up(me, p, mine)
        if ny > 1:
            to_side(me, p, mine)
        to_core(me, p, mine)

    def whole(b, sem, count):
        pieces = panel.at[b, pl.ds(0, count), pl.ds(base, users)]
        pltpu.make_async_copy(pieces, pieces, sem).wait()

    def take_core(b, p):
        piece = panel.at[b, p, pl.ds((1 - core) * users, users)]
        pltpu.make_async_copy(piece, piece, got_core.at[b, p]).wait()

    def product(b, p):
        cols = pl.ds(pl.multiple_of(p * tile, tile), tile)
        spot = pl.ds(pl.multiple_of(b * block + p * tile, tile), tile)
        co = jnp.dot(left[...], panel[b, p], preferred_element_type=jnp.float32)
        out_ref[:, spot] = co * row_damp[:, :1] * col_damp[b, :, cols]

    def own_product(p, _):
        product(me, p)
        return 0

    logs = jnp.log(counts_ref[...].astype(jnp.float32))
    col_damp[...] = jnp.exp(-0.6 * logs)
    mine = counts_ref[me, :, pl.ds(pl.multiple_of(core * half, half), half)].astype(jnp.float32)
    row_damp[...] = jnp.broadcast_to(jnp.exp(-0.4 * jnp.log(mine)), (128, half)).T
    for p in range(PIECES):
        loads[p].wait()
        take_core(me, p)
    if far:
        @pl.when(is_middle)
        def _():
            scales[...] = jnp.zeros_like(scales)

    quarter = min(256, users)

    def turned(b, target):
        def turn(c, _):
            part = pl.ds(pl.multiple_of(c * quarter, quarter), quarter)
            for j in range(half // tile):
                own = panel[b, core * (half // tile) + j, part]
                target[j * tile:(j + 1) * tile, part] = own.astype(jnp.float32).T.astype(target.dtype)
            return 0

        lax.fori_loop(0, 2 * users // quarter, turn, 0)

    turned(me, left)
    lax.fori_loop(0, PIECES, own_product, 0)

    def far_block(k):
        return far_end * ny + y + k * (ny - 1 - 2 * y)

    def sums_copy(k, c):
        return pltpu.make_async_remote_copy(
            src_ref=sums.at[k, c], dst_ref=sums.at[k, c], send_sem=sent_sums.at[k], recv_sem=got_sums.at[k],
            device_id=at(near_end, y), device_id_type=MESH)

    def scales_copy(k):
        return pltpu.make_async_remote_copy(
            src_ref=scales.at[k], dst_ref=scales.at[k], send_sem=sent_scales.at[k], recv_sem=got_scales.at[k],
            device_id=at(near_end, y), device_id_type=MESH)

    def send_sums(k, c):
        co = jnp.dot(left_far[...], panel[far_block(k), c], preferred_element_type=jnp.float32)
        most = jnp.maximum(jnp.max(co, axis=1, keepdims=True), 1e-30)
        level = (co * (2 * LEVELS / most) + 0.5).astype(jnp.int32) - LEVELS
        sums[k, c] = level.astype(jnp.int16)
        unit = jnp.broadcast_to(most * (0.5 / LEVELS), (half, 128)).T
        scales[k, pl.ds(c, 1), :] = unit[0:1]
        sums_copy(k, c).start()

        @pl.when(c == PIECES - 1)
        def _():
            scales_copy(k).start()

    def take_sums(k, _):
        b = far_end_of_end() * ny + y + k * (ny - 1 - 2 * y)
        pltpu.make_async_copy(sums.at[k], sums.at[k], got_sums.at[k]).wait()
        pltpu.make_async_copy(scales.at[k], scales.at[k], got_scales.at[k]).wait()

        def columns(c, _):
            cols = pl.ds(pl.multiple_of(c * tile, tile), tile)
            unit = jnp.broadcast_to(scales[k, pl.ds(c, 1), :], (128, half)).T
            level = sums[k, c].astype(jnp.int32) + LEVELS
            co = level.astype(jnp.float32) * unit[:, :1]
            spot = pl.ds(pl.multiple_of(b * block + c * tile, tile), tile)
            out_ref[:, spot] = co * row_damp[:, :1] * col_damp[b, :, cols]
            return 0

        lax.fori_loop(0, PIECES, columns, 0)
        return 0

    def far_end_of_end():
        return nz - 1 - z

    def distance(t):
        return jnp.where(is_middle, 3 - t, t) if far else t

    def reached(t):
        return jnp.logical_and(t >= 1, t <= reach)

    def step(s, _):
        t, p = s // PIECES, s % PIECES

        def along(zb, onward):
            b = zb * ny + y

            @pl.when(jnp.logical_and(t < reach, jnp.logical_and(zb >= 0, zb < nz)))
            def _():
                take(b, p)

                @pl.when(t + 2 <= reach)
                def _():
                    onward(b, p)

                if ny > 1:
                    across = jnp.logical_or(t > 0, is_end if far else p >= split)

                    @pl.when(across)
                    def _():
                        to_side(b, p)
                to_core(b, p)

        def multiply(b, q, k, summed):
            take_core(b, q)
            if far:
                @pl.when(jnp.logical_and(is_middle, summed))
                def _():
                    send_sums(k, q)
            product(b, q)

        def along_product(zb):
            @pl.when(jnp.logical_and(t < reach, jnp.logical_and(zb >= 0, zb < nz)))
            def _():
                multiply(zb * ny + y, p, 0, t == 1)

        along(z + 1 + t, to_down)
        along(z - 1 - t, to_up)
        if ny > 1:
            b0 = z * ny + (ny - 1 - y)

            @pl.when(t == 0)
            def _():
                take(b0, p)

                if far:
                    @pl.when(z == 0)
                    def _():
                        to_up(b0, p)

                    @pl.when(z == nz - 1)
                    def _():
                        to_down(b0, p)
                else:
                    @pl.when(p < split)
                    def _():
                        to_down(b0, p)
                        to_up(b0, p)

                to_core(b0, p)

            if far:
                @pl.when(jnp.logical_and(s == PIECES, is_middle))
                def _():
                    def inward(q, _):
                        @pl.when(z == 1)
                        def _():
                            to_up(b0, q)

                        @pl.when(z == 2)
                        def _():
                            to_down(b0, q)

                        return 0

                    lax.fori_loop(0, split, inward, 0)

                @pl.when(jnp.logical_and(s == 2 * PIECES - 1, is_middle))
                def _():
                    def late(q, _):
                        to_side((nz - 1 - z) * ny + y, q)
                        return 0

                    lax.fori_loop(split, PIECES, late, 0)

            lag = 1 if far else 0
            tc, pc = (s + PIECES - lag) // PIECES - 1, (s + PIECES - lag) % PIECES

            def crossed(zb):
                @pl.when(jnp.logical_and(reached(tc), jnp.logical_and(zb >= 0, zb < nz)))
                def _():
                    b = zb * ny + (ny - 1 - y)
                    take(b, pc)
                    to_core(b, pc)

            crossed(z + distance(tc))
            crossed(z - distance(tc))

        if far:
            @pl.when(jnp.logical_and(s == PIECES, is_middle))
            def _():
                turned(near_end * ny + y, left_far)

        along_product(z + 1 + t)
        along_product(z - 1 - t)
        if ny > 1:
            @pl.when(t == 0)
            def _():
                multiply(b0, p, 1, t > 0)

            def crossed_product(zb):
                @pl.when(jnp.logical_and(reached(tc), jnp.logical_and(zb >= 0, zb < nz)))
                def _():
                    multiply(zb * ny + (ny - 1 - y), pc, 1, tc == 1)

            crossed_product(z + distance(tc))
            crossed_product(z - distance(tc))

        return 0

    lax.fori_loop(0, (reach + 1) * PIECES + (1 if far else 0), step, 0)
    if far:
        @pl.when(is_end)
        def _():
            lax.fori_loop(0, 2, take_sums, 0)

        @pl.when(is_middle)
        def _():
            for k in range(2):
                pltpu.make_async_copy(sums.at[k], sums.at[k], sent_sums.at[k]).wait()
                pltpu.make_async_copy(scales.at[k], scales.at[k], sent_scales.at[k]).wait()

    def drain(b, _):
        zb, yb = b // ny, b % ny
        straight = yb == y
        here = jnp.logical_and(zb - z <= reach, z - zb <= reach)

        @pl.when(here)
        def _():
            whole(b, sent_core.at[b], PIECES)

        falls = jnp.logical_and(zb >= z, zb - z + 1 <= reach)
        rises = jnp.logical_and(zb <= z, z - zb + 1 <= reach)

        @pl.when(jnp.logical_and(straight, jnp.logical_and(falls, not_first)))
        def _():
            whole(b, sent_down.at[b], PIECES)

        @pl.when(jnp.logical_and(straight, jnp.logical_and(rises, not_last)))
        def _():
            whole(b, sent_up.at[b], PIECES)

        if far:
            layer = jnp.logical_and(jnp.logical_not(straight), zb == z)

            for towards, sems in ((z >= 2, sent_down), (z < 2, sent_up)):

                @pl.when(jnp.logical_and(layer, jnp.logical_and(is_end, towards)))
                def _():
                    whole(b, sems.at[b], PIECES)

                @pl.when(jnp.logical_and(layer, jnp.logical_and(is_middle, towards)))
                def _():
                    whole(b, sems.at[b], split)

            inner = jnp.logical_and(is_middle, zb == nz - 1 - z)
            outer = jnp.logical_and(is_middle, zb == near_end)
            plain = jnp.logical_not(jnp.logical_or(inner, outer))

            @pl.when(jnp.logical_and(jnp.logical_and(straight, here), plain))
            def _():
                whole(b, sent_side.at[b], PIECES)

            @pl.when(jnp.logical_and(straight, inner))
            def _():
                whole(b, sent_side.at[b], PIECES - split)

        elif ny > 1:
            layer = jnp.logical_and(jnp.logical_not(straight), zb == z)
            near = jnp.logical_or(zb == z + 1, zb == z - 1)

            @pl.when(jnp.logical_and(layer, not_first))
            def _():
                whole(b, sent_down.at[b], split)

            @pl.when(jnp.logical_and(layer, not_last))
            def _():
                whole(b, sent_up.at[b], split)

            @pl.when(jnp.logical_and(straight, near))
            def _():
                whole(b, sent_side.at[b], PIECES - split)

            @pl.when(jnp.logical_and(straight, jnp.logical_not(near)))
            def _():
                whole(b, sent_side.at[b], PIECES)

        return 0

    lax.fori_loop(0, nz * ny, drain, 0)


def shards(nz, ny, interactions, counts):
    users, block = interactions.shape
    n = nz * ny
    half = block // lax.axis_size("user")
    dma = pltpu.SemaphoreType.DMA
    tile = block // PIECES
    remote = [
        pltpu.VMEM((half, 2 * users), interactions.dtype),
        pltpu.VMEM((2, block // tile, half, tile), jnp.int16),
        pltpu.VMEM((2, 8, half), jnp.float32),
        dma((2,)),
        dma((2,)),
        dma((2,)),
        dma((2,)),
    ] if has_far(n // ny, ny) else []
    return pl.pallas_call(
        functools.partial(kernel, nz, ny),
        out_shape=pltpu.VMEM((half, n * block), jnp.float32),
        in_specs=[
            pl.BlockSpec(memory_space=pl.ANY),
            pl.BlockSpec(memory_space=pltpu.VMEM),
        ],
        out_specs=pl.BlockSpec(memory_space=pltpu.VMEM),
        scratch_shapes=[
            pltpu.VMEM((n, PIECES, 2 * users, block // PIECES), interactions.dtype),
            pltpu.VMEM((half, 2 * users), interactions.dtype),
            pltpu.VMEM((half, 128), jnp.float32),
            pltpu.VMEM((n, 1, block), jnp.float32),
            dma((n, PIECES)),
            dma((n, PIECES)),
            dma((n,)),
            dma((n,)),
            dma((n,)),
            dma((n,)),
            dma((PIECES,)),
            *remote,
        ],
        compiler_params=pltpu.CompilerParams(
            collective_id=0, has_side_effects=True, vmem_limit_bytes=(44 if remote else 40) * 1024 * 1024
        ),
        cost_estimate=pl.CostEstimate(
            flops=4 * half * users * n * block, bytes_accessed=4 * half * n * block, transcendentals=0
        ),
    )(interactions, counts.reshape(n, 1, block))


def columns_of(mesh):
    n = mesh.shape["item"]
    spots = [getattr(d, "coords", None) for d in mesh.devices[0, :, 0]]
    if any(spot is None for spot in spots):
        return 1
    ny = len({spot[1] for spot in spots})
    return ny if ny == 2 and n % 2 == 0 else 1


def solution(mesh):
    ny = columns_of(mesh)
    placed = (P(("groups", "user"), "item"), P("groups"))
    return jax.shard_map(
        functools.partial(shards, mesh.shape["item"] // ny, ny),
        mesh=mesh,
        in_specs=placed,
        out_specs=P(("groups", "item", "user"), None),
        check_vma=False,
    )
```

```python
import functools

import jax
import jax.numpy as jnp
from jax import lax
from jax.experimental import pallas as pl
from jax.experimental.pallas import tpu as pltpu
from jax.sharding import PartitionSpec as P

MESH = pl.DeviceIdType.MESH
PIECES = 4
LEVELS = 32767


def has_far(nz, ny):
    return nz == 4 and ny == 2


def kernel(nz, ny, x_ref, counts_ref, out_ref, panel, left, row_damp, col_damp,
           got, got_core, sent_down, sent_up, sent_side, sent_core, loaded, *remote):
    users, block = x_ref.shape
    half = out_ref.shape[0]
    tile = block // PIECES
    split = PIECES // 2
    group = lax.axis_index("groups")
    me = lax.axis_index("item")
    core = lax.axis_index("user")
    z, y = me // ny, me % ny
    base = core * users

    def at(zz, yy):
        return (group, zz * ny + yy, core)

    down, up, side = at(z - 1, y), at(z + 1, y), at(z, ny - 1 - y)
    other = (group, me, 1 - core)
    not_first, not_last = z > 0, z < nz - 1
    far = has_far(nz, ny)
    reach = nz - 2 if far else nz - 1
    is_end = jnp.logical_or(z == 0, z == nz - 1)
    is_middle = jnp.logical_not(is_end)
    near_end = jnp.where(z < 2, 0, nz - 1)
    far_end = nz - 1 - near_end
    if far:
        left_far, sums, scales, sent_sums, got_sums, sent_scales, got_scales = remote

    barrier = pltpu.get_barrier_semaphore()
    pl.semaphore_signal(barrier, inc=1, device_id=other, device_id_type=MESH)
    if ny > 1:
        pl.semaphore_signal(barrier, inc=1, device_id=side, device_id_type=MESH)

    @pl.when(not_first)
    def _():
        pl.semaphore_signal(barrier, inc=1, device_id=down, device_id_type=MESH)

    @pl.when(not_last)
    def _():
        pl.semaphore_signal(barrier, inc=1, device_id=up, device_id_type=MESH)

    loads = [
        pltpu.make_async_copy(x_ref.at[:, pl.ds(p * tile, tile)], panel.at[me, p, pl.ds(base, users)], loaded.at[p])
        for p in range(PIECES)
    ]
    for load in loads:
        load.start()
    wanted = ny + jnp.where(not_first, 1, 0) + jnp.where(not_last, 1, 0)
    pl.semaphore_wait(barrier, wanted)

    def place(b, p):
        return panel.at[b, p, pl.ds(base, users)]

    def send(b, p, sems, recv, device, source=None):
        pltpu.make_async_remote_copy(
            src_ref=place(b, p) if source is None else source,
            dst_ref=place(b, p),
            send_sem=sems.at[b],
            recv_sem=recv,
            device_id=device,
            device_id_type=MESH,
        ).start()

    def take(b, p):
        pltpu.make_async_copy(place(b, p), place(b, p), got.at[b, p]).wait()

    def to_down(b, p, source=None):
        @pl.when(not_first)
        def _():
            send(b, p, sent_down, got.at[b, p], down, source)

    def to_up(b, p, source=None):
        @pl.when(not_last)
        def _():
            send(b, p, sent_up, got.at[b, p], up, source)

    def to_side(b, p, source=None):
        send(b, p, sent_side, got.at[b, p], side, source)

    def to_core(b, p, source=None):
        send(b, p, sent_core, got_core.at[b, p], other, source)

    for p in range(PIECES):
        mine = x_ref.at[:, pl.ds(p * tile, tile)]
        to_down(me, p, mine)
        to_up(me, p, mine)
        if ny > 1:
            to_side(me, p, mine)
        to_core(me, p, mine)

    def whole(b, sem, count):
        pieces = panel.at[b, pl.ds(0, count), pl.ds(base, users)]
        pltpu.make_async_copy(pieces, pieces, sem).wait()

    def take_core(b, p):
        piece = panel.at[b, p, pl.ds((1 - core) * users, users)]
        pltpu.make_async_copy(piece, piece, got_core.at[b, p]).wait()

    def product(b, p):
        cols = pl.ds(pl.multiple_of(p * tile, tile), tile)
        spot = pl.ds(pl.multiple_of(b * block + p * tile, tile), tile)
        co = jnp.dot(left[...], panel[b, p], preferred_element_type=jnp.float32)
        out_ref[:, spot] = co * row_damp[:, :1] * col_damp[b, :, cols]

    def own_product(p, _):
        product(me, p)
        return 0

    logs = jnp.log(counts_ref[...].astype(jnp.float32))
    col_damp[...] = jnp.exp(-0.6 * logs)
    mine = counts_ref[me, :, pl.ds(pl.multiple_of(core * half, half), half)].astype(jnp.float32)
    row_damp[...] = jnp.broadcast_to(jnp.exp(-0.4 * jnp.log(mine)), (128, half)).T
    for p in range(PIECES):
        loads[p].wait()
        take_core(me, p)
    quarter = min(256, users)

    def turned(b, target):
        def turn(c, _):
            part = pl.ds(pl.multiple_of(c * quarter, quarter), quarter)
            for j in range(half // tile):
                own = panel[b, core * (half // tile) + j, part]
                target[j * tile:(j + 1) * tile, part] = own.astype(jnp.float32).T.astype(target.dtype)
            return 0

        lax.fori_loop(0, 2 * users // quarter, turn, 0)

    turned(me, left)
    lax.fori_loop(0, PIECES, own_product, 0)

    def far_block(k):
        return far_end * ny + y + k * (ny - 1 - 2 * y)

    def sums_copy(k, c):
        return pltpu.make_async_remote_copy(
            src_ref=sums.at[k, c], dst_ref=sums.at[k, c], send_sem=sent_sums.at[k], recv_sem=got_sums.at[k, c],
            device_id=at(near_end, y), device_id_type=MESH)

    def scales_copy(k, c):
        return pltpu.make_async_remote_copy(
            src_ref=scales.at[k, c], dst_ref=scales.at[k, c], send_sem=sent_scales.at[k],
            recv_sem=got_scales.at[k, c], device_id=at(near_end, y), device_id_type=MESH)

    def send_sums(k, c):
        co = jnp.dot(left_far[...], panel[far_block(k), c], preferred_element_type=jnp.float32)
        most = jnp.maximum(jnp.max(co, axis=1, keepdims=True), 1e-30)
        level = (co * (2 * LEVELS / most) + 0.5).astype(jnp.int32) - LEVELS
        sums[k, c] = level.astype(jnp.int16)
        unit = jnp.broadcast_to(most * (0.5 / LEVELS), (half, 128)).T
        scales[k, c] = unit[0:1]
        scales_copy(k, c).start()
        sums_copy(k, c).start()

    def take_sums(k, c):
        b = far_end_of_end() * ny + y + k * (ny - 1 - 2 * y)
        pltpu.make_async_copy(scales.at[k, c], scales.at[k, c], got_scales.at[k, c]).wait()
        pltpu.make_async_copy(sums.at[k, c], sums.at[k, c], got_sums.at[k, c]).wait()
        cols = pl.ds(pl.multiple_of(c * tile, tile), tile)
        unit = jnp.broadcast_to(scales[k, c], (128, half)).T
        level = sums[k, c].astype(jnp.int32) + LEVELS
        co = level.astype(jnp.float32) * unit[:, :1]
        spot = pl.ds(pl.multiple_of(b * block + c * tile, tile), tile)
        out_ref[:, spot] = co * row_damp[:, :1] * col_damp[b, :, cols]

    def far_end_of_end():
        return nz - 1 - z

    def distance(t):
        return jnp.where(is_middle, 3 - t, t) if far else t

    def reached(t):
        return jnp.logical_and(t >= 1, t <= reach)

    def step(s, _):
        t, p = s // PIECES, s % PIECES

        def along(zb, onward):
            b = zb * ny + y

            @pl.when(jnp.logical_and(t < reach, jnp.logical_and(zb >= 0, zb < nz)))
            def _():
                take(b, p)

                @pl.when(t + 2 <= reach)
                def _():
                    onward(b, p)

                if ny > 1:
                    across = jnp.logical_or(t > 0, is_end if far else p >= split)

                    @pl.when(across)
                    def _():
                        to_side(b, p)
                to_core(b, p)

        def multiply(b, q, k, summed):
            take_core(b, q)
            if far:
                @pl.when(jnp.logical_and(is_middle, summed))
                def _():
                    send_sums(k, q)
            product(b, q)

        def along_product(zb):
            @pl.when(jnp.logical_and(t < reach, jnp.logical_and(zb >= 0, zb < nz)))
            def _():
                multiply(zb * ny + y, p, 0, t == 1)

        along(z + 1 + t, to_down)
        along(z - 1 - t, to_up)
        if ny > 1:
            b0 = z * ny + (ny - 1 - y)

            @pl.when(t == 0)
            def _():
                take(b0, p)

                if far:
                    @pl.when(z == 0)
                    def _():
                        to_up(b0, p)

                    @pl.when(z == nz - 1)
                    def _():
                        to_down(b0, p)
                else:
                    @pl.when(p < split)
                    def _():
                        to_down(b0, p)
                        to_up(b0, p)

                to_core(b0, p)

            if far:
                @pl.when(jnp.logical_and(s == PIECES, is_middle))
                def _():
                    def inward(q, _):
                        @pl.when(z == 1)
                        def _():
                            to_up(b0, q)

                        @pl.when(z == 2)
                        def _():
                            to_down(b0, q)

                        return 0

                    lax.fori_loop(0, split, inward, 0)

                @pl.when(jnp.logical_and(s == 2 * PIECES - 1, is_middle))
                def _():
                    def late(q, _):
                        to_side((nz - 1 - z) * ny + y, q)
                        return 0

                    lax.fori_loop(split, PIECES, late, 0)

            lag = 1 if far else 0
            tc, pc = (s + PIECES - lag) // PIECES - 1, (s + PIECES - lag) % PIECES

            def crossed(zb):
                @pl.when(jnp.logical_and(reached(tc), jnp.logical_and(zb >= 0, zb < nz)))
                def _():
                    b = zb * ny + (ny - 1 - y)
                    take(b, pc)
                    to_core(b, pc)

            crossed(z + distance(tc))
            crossed(z - distance(tc))

        if far:
            @pl.when(jnp.logical_and(s == PIECES, is_middle))
            def _():
                turned(near_end * ny + y, left_far)

        along_product(z + 1 + t)
        along_product(z - 1 - t)
        if ny > 1:
            @pl.when(t == 0)
            def _():
                multiply(b0, p, 1, t > 0)

            def crossed_product(zb):
                @pl.when(jnp.logical_and(reached(tc), jnp.logical_and(zb >= 0, zb < nz)))
                def _():
                    multiply(zb * ny + (ny - 1 - y), pc, 1, tc == 1)

            crossed_product(z + distance(tc))
            crossed_product(z - distance(tc))

        if far:
            @pl.when(jnp.logical_and(is_end, tc == 2))
            def _():
                take_sums(0, pc)
                take_sums(1, pc)

        return 0

    lax.fori_loop(0, (reach + 1) * PIECES + (1 if far else 0), step, 0)
    if far:
        @pl.when(is_middle)
        def _():
            for k in range(2):
                pltpu.make_async_copy(sums.at[k], sums.at[k], sent_sums.at[k]).wait()
                pltpu.make_async_copy(scales.at[k], scales.at[k], sent_scales.at[k]).wait()

    def drain(b, _):
        zb, yb = b // ny, b % ny
        straight = yb == y
        here = jnp.logical_and(zb - z <= reach, z - zb <= reach)

        @pl.when(here)
        def _():
            whole(b, sent_core.at[b], PIECES)

        falls = jnp.logical_and(zb >= z, zb - z + 1 <= reach)
        rises = jnp.logical_and(zb <= z, z - zb + 1 <= reach)

        @pl.when(jnp.logical_and(straight, jnp.logical_and(falls, not_first)))
        def _():
            whole(b, sent_down.at[b], PIECES)

        @pl.when(jnp.logical_and(straight, jnp.logical_and(rises, not_last)))
        def _():
            whole(b, sent_up.at[b], PIECES)

        if far:
            layer = jnp.logical_and(jnp.logical_not(straight), zb == z)

            for towards, sems in ((z >= 2, sent_down), (z < 2, sent_up)):

                @pl.when(jnp.logical_and(layer, jnp.logical_and(is_end, towards)))
                def _():
                    whole(b, sems.at[b], PIECES)

                @pl.when(jnp.logical_and(layer, jnp.logical_and(is_middle, towards)))
                def _():
                    whole(b, sems.at[b], split)

            inner = jnp.logical_and(is_middle, zb == nz - 1 - z)
            outer = jnp.logical_and(is_middle, zb == near_end)
            plain = jnp.logical_not(jnp.logical_or(inner, outer))

            @pl.when(jnp.logical_and(jnp.logical_and(straight, here), plain))
            def _():
                whole(b, sent_side.at[b], PIECES)

            @pl.when(jnp.logical_and(straight, inner))
            def _():
                whole(b, sent_side.at[b], PIECES - split)

        elif ny > 1:
            layer = jnp.logical_and(jnp.logical_not(straight), zb == z)
            near = jnp.logical_or(zb == z + 1, zb == z - 1)

            @pl.when(jnp.logical_and(layer, not_first))
            def _():
                whole(b, sent_down.at[b], split)

            @pl.when(jnp.logical_and(layer, not_last))
            def _():
                whole(b, sent_up.at[b], split)

            @pl.when(jnp.logical_and(straight, near))
            def _():
                whole(b, sent_side.at[b], PIECES - split)

            @pl.when(jnp.logical_and(straight, jnp.logical_not(near)))
            def _():
                whole(b, sent_side.at[b], PIECES)

        return 0

    lax.fori_loop(0, nz * ny, drain, 0)


def shards(nz, ny, interactions, counts):
    users, block = interactions.shape
    n = nz * ny
    half = block // lax.axis_size("user")
    dma = pltpu.SemaphoreType.DMA
    tile = block // PIECES
    remote = [
        pltpu.VMEM((half, 2 * users), interactions.dtype),
        pltpu.VMEM((2, block // tile, half, tile), jnp.int16),
        pltpu.VMEM((2, PIECES, 1, half), jnp.float32),
        dma((2,)),
        dma((2, PIECES)),
        dma((2,)),
        dma((2, PIECES)),
    ] if has_far(n // ny, ny) else []
    return pl.pallas_call(
        functools.partial(kernel, nz, ny),
        out_shape=pltpu.VMEM((half, n * block), jnp.float32),
        in_specs=[
            pl.BlockSpec(memory_space=pl.ANY),
            pl.BlockSpec(memory_space=pltpu.VMEM),
        ],
        out_specs=pl.BlockSpec(memory_space=pltpu.VMEM),
        scratch_shapes=[
            pltpu.VMEM((n, PIECES, 2 * users, block // PIECES), interactions.dtype),
            pltpu.VMEM((half, 2 * users), interactions.dtype),
            pltpu.VMEM((half, 128), jnp.float32),
            pltpu.VMEM((n, 1, block), jnp.float32),
            dma((n, PIECES)),
            dma((n, PIECES)),
            dma((n,)),
            dma((n,)),
            dma((n,)),
            dma((n,)),
            dma((PIECES,)),
            *remote,
        ],
        compiler_params=pltpu.CompilerParams(
            collective_id=0, has_side_effects=True, vmem_limit_bytes=(44 if remote else 40) * 1024 * 1024
        ),
        cost_estimate=pl.CostEstimate(
            flops=4 * half * users * n * block, bytes_accessed=4 * half * n * block, transcendentals=0
        ),
    )(interactions, counts.reshape(n, 1, block))


def columns_of(mesh):
    n = mesh.shape["item"]
    spots = [getattr(d, "coords", None) for d in mesh.devices[0, :, 0]]
    if any(spot is None for spot in spots):
        return 1
    ny = len({spot[1] for spot in spots})
    return ny if ny == 2 and n % 2 == 0 else 1


def solution(mesh):
    ny = columns_of(mesh)
    placed = (P(("groups", "user"), "item"), P("groups"))
    return jax.shard_map(
        functools.partial(shards, mesh.shape["item"] // ny, ny),
        mesh=mesh,
        in_specs=placed,
        out_specs=P(("groups", "item", "user"), None),
        check_vma=False,
    )
```
